256 devices in a mesh: tp: 8 (over z), ep: 32 (over x, y, core).
Axes of the slice: x: 4, y: 4, z: 8, core: 2. Of those that a mesh axis runs over, the one named last changes fastest.
Arguments:
- tokens: bfloat16 [4096, 7168], P('ep', 'tp'), may hold values from -6 to 6
- indices: int32 [4096, 8], P('ep'), may hold values from 0 to 31, all different within a row
- scores: float32 [4096, 8], P('ep'), may hold values from 0.05 to 1
- gate_weight: bfloat16 [32, 7168, 2048], P('ep', None, 'tp'), may hold values from -0.0625 to 0.0625
- up_weight: bfloat16 [32, 7168, 2048], P('ep', None, 'tp'), may hold values from -0.0625 to 0.0625
- down_weight: bfloat16 [32, 7168, 2048], P('ep', 'tp'), may hold values from -0.125 to 0.125
Outputs:
- mixed: bfloat16 [4096, 7168], P('ep', 'tp')
The draws below stay inside these ranges and needn't reach their ends.
Inputs may be any that keep to these rules, and one draw needn't show every extreme that they name: `indices`: each token names 8 different experts; every expert is named by some token.
All inputs are finite; a program needn't handle non-finite values.
Results may differ from the reference program's by a relative error of at most 0.0057.
Values may be sent and summed in bfloat16 or wider, within the bound.
A program may use at most 128 MiB of HBM per device.

```python
import jax
import jax.numpy as jnp
from jax import lax

D = 7168
EXP_HID = 2048
TOPK = 8
TOK_DEV = 128
EXPERTS = 32
TOKENS = 4096
CAP = 32
N_EP = 32


def steps_of(own_key, extent, cuts, smallest, high):
    gain = 1.0
    for axis_at, parts in cuts:
        steps = jax.random.uniform(jax.random.fold_in(jax.random.fold_in(own_key, 6), axis_at), (parts,), jnp.float32, smallest / len(cuts), high / len(cuts))
        gain = gain * jnp.repeat(jnp.exp(steps), extent[axis_at] // parts).reshape((-1,) + (1,) * (len(extent) - 1 - axis_at))
    return gain


def different_ones(own_key, rows, count, top, lift):
    order = jax.random.permutation(jax.random.fold_in(own_key, 1), count)
    boost = order
    for power in range(3):
        boost = boost * boost // count
    boost = boost * lift // count
    chance = jax.random.randint(jax.random.fold_in(own_key, 2), (rows, count), 0, 4096) + boost
    holders = jax.random.permutation(jax.random.fold_in(own_key, 3), rows)[jnp.arange(count) % rows]
    chance = jnp.where(jnp.arange(rows)[:, None] == holders[None, :], 1 << 14, chance)
    priority = chance * count + jnp.arange(count)
    return lax.top_k(priority.astype(jnp.int32), top)[1].astype(jnp.int32)


def centred(rng, extent, deviation, reach, split=(), held_as=jnp.bfloat16):
    level = steps_of(rng, extent, split, -0.22, 0.18) if split else 1.0
    result = jax.random.normal(rng, extent, jnp.float32) * deviation * level
    return jnp.minimum(jnp.maximum(result, -reach), reach).astype(held_as)


def setup_inputs(seed: int = 0) -> dict:
    splits = jax.random.split(jax.random.key(seed), 7)
    return {
        "tokens": centred(splits[0], (TOKENS, D), 1.0, 6.0, ((0, 32), (1, 8))),
        "indices": different_ones(splits[1], TOKENS, EXPERTS, TOPK, 2048),
        "scores": jnp.clip(0.05 + 0.95 * jax.random.uniform(splits[2], (TOKENS, TOPK), jnp.float32) ** steps_of(splits[2], (TOKENS, TOPK), ((0, 32),), -0.2, 0.2), 0.05, 1.0),
        "gate_weight": centred(splits[3], (EXPERTS, D, EXP_HID), D ** -0.5, 0.0625, ((0, 32), (2, 8))),
        "up_weight": centred(splits[4], (EXPERTS, D, EXP_HID), D ** -0.5, 0.0625, ((0, 32), (2, 8))),
        "down_weight": centred(splits[5], (EXPERTS, D, EXP_HID), EXP_HID ** -0.5, 0.125, ((0, 32), (1, 8))),
    }


def place(index_block, experts, capacity):
    flattened = index_block.reshape(-1)
    onehot = (flattened[:, None] == jnp.arange(experts, dtype=jnp.int32)[None, :]).astype(jnp.int32)
    earlier = jnp.cumsum(onehot, axis=0) - onehot
    position = jnp.sum(earlier * onehot, axis=1).astype(jnp.int32)
    retained = position < capacity
    target = jnp.where(retained, flattened * capacity + position, experts * capacity).astype(jnp.int32)
    return target, retained


def reference(tokens, indices, scores, gate_weight, up_weight, down_weight):
    blocks = indices.reshape(N_EP, TOK_DEV, TOPK)
    target, retained = jax.vmap(lambda one_block: place(one_block, EXPERTS, CAP))(blocks)
    owner_row = jnp.arange(TOK_DEV * TOPK, dtype=jnp.int32) // TOPK

    def tables(one_target):
        slot_token = jnp.zeros((EXPERTS * CAP,), jnp.int32).at[one_target].set(owner_row, mode="drop")
        slot_valid = jnp.zeros((EXPERTS * CAP,), jnp.int32).at[one_target].set(1, mode="drop")
        return slot_token, slot_valid

    slot_token, slot_valid = jax.vmap(tables)(target)
    global_row = slot_token + (jnp.arange(N_EP, dtype=jnp.int32) * TOK_DEV)[:, None]
    rows_index = global_row.reshape(N_EP, EXPERTS, CAP).transpose(1, 0, 2).reshape(EXPERTS, N_EP * CAP)
    rows_valid = slot_valid.reshape(N_EP, EXPERTS, CAP).transpose(1, 0, 2).reshape(EXPERTS, N_EP * CAP)

    def expert(operands):
        row_index, row_valid, w_gate, w_up, w_down = operands
        expert_rows = jnp.where(row_valid[:, None] > 0, tokens[row_index], jnp.zeros((), jnp.bfloat16))
        gate = jnp.dot(expert_rows, w_gate, preferred_element_type=jnp.float32)
        upward = jnp.dot(expert_rows, w_up, preferred_element_type=jnp.float32)
        hidden = (jax.nn.silu(gate) * upward).astype(jnp.bfloat16)
        total = jnp.dot(hidden, w_down.T, preferred_element_type=jnp.float32)
        return total.astype(jnp.bfloat16)

    expert_out = lax.map(expert, (rows_index, rows_valid, gate_weight, up_weight, down_weight))
    returned = expert_out.reshape(EXPERTS, N_EP, CAP, D).transpose(1, 0, 2, 3).reshape(N_EP, EXPERTS * CAP, D)
    route = 2.5 * scores / jnp.sum(scores, axis=1, keepdims=True)
    route = jnp.where(retained, route.reshape(N_EP, TOK_DEV * TOPK), 0.0)

    def combine(operands):
        one_back, one_target, one_route = operands
        picked = one_back[jnp.minimum(one_target, EXPERTS * CAP - 1)].astype(jnp.float32)
        weighted = picked * one_route[:, None]
        return jnp.sum(weighted.reshape(TOK_DEV, TOPK, D), axis=1).astype(jnp.bfloat16)

    mixed = lax.map(combine, (returned, target, route))
    return mixed.reshape(TOKENS, D)
```

```python
import functools

import jax
import jax.numpy as jnp
from jax import lax
from jax.experimental import pallas as pl
from jax.experimental.pallas import tpu as pltpu
from jax.sharding import PartitionSpec as P

MESH = pl.DeviceIdType.MESH
BF16 = jnp.bfloat16
F32 = jnp.float32
TP = 8
CAP = 32
TOK = 128
FEAT = 896
HID = 256
CHUNKS = 8
BLOCKS = 4
ROWS = BLOCKS * CAP
TOPK = 8
PEERS = CHUNKS * BLOCKS
DIRECT = (0, 2, 6, 4)
TOKEN_SHIFTS = (2, 6, 4)


def dot(a, b):
    return jnp.dot(a, b, preferred_element_type=F32)


def kernel(
    idx_ref, score_ref, tok_in, gate_hbm, up_hbm, down_hbm,
    out_ref,
    w_gate, w_up, w_down, pick, route, tok, outgoing, x, acc_gate, acc_up, hid, res, ret, mix,
    w_sem, tok_send, tok_recv, x_send, x_recv, fwd_send, hid_send, hid_recv, half_recv, ret_send, ret_recv,
):
    z = lax.axis_index("tp")
    e = lax.axis_index("ep")
    ex, ey, ec = lax.div(e, 8), lax.rem(lax.div(e, 2), 4), lax.rem(e, 2)

    def plane(shift):
        return lax.rem(z + shift, TP)

    def peer(c, b, sign):
        dx = lax.div(c, 4) + 2 * (b // 2)
        dy = lax.rem(c, 4) + 2 * (b // 2)
        px = lax.rem(ex + sign * dx + 4, 4)
        py = lax.rem(ey + sign * dy + 8, 4)
        pc = lax.rem(ec + b % 2, 2)
        return (z, (px * 4 + py) * 2 + pc)

    barrier = pltpu.get_barrier_semaphore()

    def greet(c, _):
        for b in range(BLOCKS):
            if b == 0:
                @pl.when(c > 0)
                def _():
                    pl.semaphore_signal(barrier, inc=1, device_id=peer(c, b, 1), device_id_type=MESH)
            else:
                pl.semaphore_signal(barrier, inc=1, device_id=peer(c, b, 1), device_id_type=MESH)
        return 0

    lax.fori_loop(0, CHUNKS, greet, 0)
    for shift in (1, 7, 2, 6, 4):
        pl.semaphore_signal(barrier, inc=1, device_id=(plane(shift), e), device_id_type=MESH)

    weights = [
        pltpu.make_async_copy(gate_hbm, w_gate, w_sem.at[0]),
        pltpu.make_async_copy(up_hbm, w_up, w_sem.at[1]),
        pltpu.make_async_copy(down_hbm, w_down, w_sem.at[2]),
    ]
    for copy in weights:
        copy.start()

    lane = lax.broadcasted_iota(jnp.int32, (TOK, 128), 1)
    row = lax.broadcasted_iota(jnp.int32, (TOK, 128), 0)
    far = 2 * ((lane >> 1) & 1)
    at_x = (ex + ((lane >> 4) & 1) + far) & 3
    at_y = (ey + ((lane >> 2) & 3) + far) & 3
    at_c = (ec + lane) & 1
    expert = jnp.where(lane < PEERS, (at_x * 4 + at_y) * 2 + at_c, -1)
    scores = score_ref[...]
    share = 2.5 * scores / jnp.sum(scores, axis=1, keepdims=True)
    chosen = jnp.zeros((TOK, 128), F32)
    weight = jnp.zeros((TOK, 128), F32)
    for j in range(TOPK):
        hit = idx_ref[:, j : j + 1] == expert
        chosen = jnp.where(hit, 1.0, chosen)
        weight = jnp.where(hit, share[:, j : j + 1], weight)
    before = jnp.where(lane < row, 1.0, 0.0).astype(BF16)
    position = dot(before, chosen.astype(BF16))
    slot = jnp.where(chosen > 0.5, position, -1.0)
    slot_t = slot.T
    place = lax.broadcasted_iota(jnp.int32, (CAP, TOK), 0).astype(F32)
    for k in range(PEERS):
        pick[k // BLOCKS, (k % BLOCKS) * CAP : (k % BLOCKS + 1) * CAP, :] = jnp.where(
            slot_t[k : k + 1, :] == place, 1.0, 0.0
        ).astype(BF16)

    pl.semaphore_wait(barrier, PEERS - 1 + 5)

    def token_copy(n):
        shift = TOKEN_SHIFTS[n]
        return pltpu.make_async_remote_copy(
            src_ref=tok_in, dst_ref=tok.at[n], send_sem=tok_send.at[n], recv_sem=tok_recv.at[n],
            device_id=(plane(TP - shift), e), device_id_type=MESH,
        )

    for n in range(3):
        token_copy(n).start()

    def dispatch(n, c):
        d = DIRECT[n]
        source = tok_in[...] if n == 0 else tok[n - 1]
        outgoing[n, c] = dot(pick[c], source).astype(BF16)
        for b in range(BLOCKS):
            rows = pl.ds(b * CAP, CAP)

            def remote():
                pltpu.make_async_remote_copy(
                    src_ref=outgoing.at[n, c, rows], dst_ref=x.at[d, c, rows],
                    send_sem=x_send.at[n, c], recv_sem=x_recv.at[d, c],
                    device_id=peer(c, b, 1), device_id_type=MESH,
                ).start()

            def own():
                pltpu.make_async_copy(outgoing.at[n, c, rows], x.at[d, c, rows], x_recv.at[d, c]).start()

            if b == 0:
                pl.when(c > 0)(remote)
                pl.when(c == 0)(own)
            else:
                remote()

    def wait(ref, sem):
        pltpu.make_async_copy(ref, ref, sem).wait()

    def arrived(d, c):
        wait(x.at[d, c], x_recv.at[d, c])

    def hand_on(d, c, step, n):
        there = (d - step) % TP
        pltpu.make_async_remote_copy(
            src_ref=x.at[d, c], dst_ref=x.at[there, c],
            send_sem=fwd_send.at[n, c], recv_sem=x_recv.at[there, c],
            device_id=(plane(step % TP), e), device_id_type=MESH,
        ).start()

    def gate_up(c, offsets, gate, up):
        for d in offsets:
            rows = x[d, c]
            at = plane(d)
            g, u = dot(rows, w_gate[at]), dot(rows, w_up[at])
            gate = g if gate is None else gate + g
            up = u if up is None else up + u
        return gate, up

    def hid_copy(src, c, shift, n, half=None):
        rows = pl.ds(0, ROWS) if half is None else pl.ds(half * (ROWS // 2), ROWS // 2)
        recv = half_recv.at[half, c] if half is not None else hid_recv.at[src, c]
        pltpu.make_async_remote_copy(
            src_ref=hid.at[src, c, rows], dst_ref=hid.at[src, c, rows],
            send_sem=hid_send.at[n, c], recv_sem=recv,
            device_id=(plane(shift), e), device_id_type=MESH,
        ).start()

    def hid_wait(src, c):
        wait(hid.at[src, c], hid_recv.at[src, c])

    def first_half(c):
        gate, up = gate_up(c, (0, 2, 6), None, None)
        acc_gate[...] = gate
        acc_up[...] = up

    def second_half(c):
        for d in (4, 1, 7, 3, 5):
            arrived(d, c)
        gate, up = gate_up(c, (4, 1, 7, 3, 5), acc_gate[...], acc_up[...])
        hid[z, c] = (gate / (1.0 + jnp.exp(-gate)) * up).astype(BF16)
        hid_copy(z, c, 1, 0)
        hid_copy(z, c, 7, 1)

    def second_hop(c):
        hid_wait(plane(7), c)
        hid_copy(plane(7), c, 1, 2)
        hid_wait(plane(1), c)
        hid_copy(plane(1), c, 7, 3)

    def third_hop(c):
        hid_wait(plane(6), c)
        hid_copy(plane(6), c, 1, 4)
        hid_copy(plane(6), c, 2, 5, half=0)
        hid_wait(plane(2), c)
        hid_copy(plane(2), c, 7, 6)
        hid_copy(plane(2), c, 6, 7, half=1)

    def ret_block(c, b):
        rows = pl.ds(b * CAP, CAP)

        def remote():
            pltpu.make_async_remote_copy(
                src_ref=res.at[c, rows], dst_ref=ret.at[c, rows],
                send_sem=ret_send.at[c], recv_sem=ret_recv.at[c],
                device_id=peer(c, b, -1), device_id_type=MESH,
            ).start()

        def own():
            pltpu.make_async_copy(res.at[c, rows], ret.at[c, rows], ret_recv.at[c]).start()

        if b == 0:
            pl.when(c > 0)(remote)
            pl.when(c == 0)(own)
        else:
            remote()

    def down(c):
        hid_wait(plane(5), c)
        hid_wait(plane(3), c)
        for half in range(2):
            rows = pl.ds(half * (ROWS // 2), ROWS // 2)
            wait(hid.at[plane(4), c, rows], half_recv.at[half, c])
        total = None
        for s in range(TP):
            part = lax.dot_general(
                hid[s, c], w_down[:, s * HID : (s + 1) * HID], (((1,), (1,)), ((), ())),
                preferred_element_type=F32,
            )
            total = part if total is None else total + part
        res[c] = total.astype(BF16)
        for b in range(BLOCKS):
            ret_block(c, b)

    def combine(c):
        wait(ret.at[c], ret_recv.at[c])
        rows = ret[c]
        mix[...] += dot(route[0, c], rows) + dot(route[1, c], rows) + dot(route[2, c], rows)

    for c in range(3):
        dispatch(0, c)

    high = weight.astype(BF16)
    rest = weight - high.astype(F32)
    middle = rest.astype(BF16)
    low = (rest - middle.astype(F32)).astype(BF16)
    slot_b = slot.astype(BF16)

    def spread(c, _):
        take = jnp.where(row == c * BLOCKS + (lane >> 5), 1.0, 0.0).astype(BF16)
        here = dot(slot_b, take) == (lane & (CAP - 1)).astype(F32)
        for n, part in enumerate((high, middle, low)):
            route[n, c] = jnp.where(here, dot(part, take), 0.0).astype(BF16)
        return 0

    lax.fori_loop(0, CHUNKS, spread, 0)
    mix[...] = jnp.zeros_like(mix)

    for n in (1, 2):
        wait(tok.at[n - 1], tok_recv.at[n - 1])
        dispatch(n, 0)
    for copy in weights:
        copy.wait()

    def step(j, _):
        def at(lag, do):
            c = j - lag
            pl.when(jnp.logical_and(c >= 0, c < CHUNKS))(lambda: do(c))

        def own_slice(c):
            arrived(0, c)
            hand_on(0, c, 1, 0)
            hand_on(0, c, -1, 1)

        def other_slices(c):
            arrived(2, c)
            hand_on(2, c, -1, 2)
            arrived(6, c)
            hand_on(6, c, 1, 3)

        @pl.when(j == 0)
        def _():
            wait(tok.at[2], tok_recv.at[2])

        at(1, second_half)
        at(0, own_slice)
        at(0, lambda c: dispatch(3, c))
        at(1, second_hop)
        at(-3, lambda c: dispatch(0, c))
        at(-1, lambda c: dispatch(1, c))
        at(-1, lambda c: dispatch(2, c))
        at(0, other_slices)
        at(2, down)
        at(0, first_half)
        at(1, third_hop)
        at(3, combine)
        return 0

    lax.fori_loop(0, CHUNKS + 3, step, 0)

    out_ref[...] = mix[...].astype(BF16)

    for n in range(3):
        wait(tok_in, tok_send.at[n])

    def drain(c, _):
        for n in range(4):
            @pl.when(c > 0)
            def _():
                wait(outgoing.at[n, c], x_send.at[n, c])

            @pl.when(c == 0)
            def _():
                part = outgoing.at[n, c, pl.ds(CAP, ROWS - CAP)]
                wait(part, x_send.at[n, c])

            wait(x.at[0, c], fwd_send.at[n, c])
        for n in range(8):
            if n in (5, 7):
                half = hid.at[0, c, pl.ds(0, ROWS // 2)]
                wait(half, hid_send.at[n, c])
            else:
                wait(hid.at[0, c], hid_send.at[n, c])

        @pl.when(c > 0)
        def _():
            wait(res.at[c], ret_send.at[c])

        @pl.when(c == 0)
        def _():
            part = res.at[c, pl.ds(CAP, ROWS - CAP)]
            wait(part, ret_send.at[c])

        return 0

    lax.fori_loop(0, CHUNKS, drain, 0)


def local(tokens, indices, scores, gate_weight, up_weight, down_weight):
    vmem = pl.BlockSpec(memory_space=pltpu.VMEM)
    anywhere = pl.BlockSpec(memory_space=pl.ANY)
    dma = pltpu.SemaphoreType.DMA
    return pl.pallas_call(
        kernel,
        out_shape=jax.ShapeDtypeStruct((TOK, FEAT), BF16),
        in_specs=[vmem, vmem, vmem, anywhere, anywhere, anywhere],
        out_specs=vmem,
        scratch_shapes=[
            pltpu.VMEM((TP, FEAT, HID), BF16),
            pltpu.VMEM((TP, FEAT, HID), BF16),
            pltpu.VMEM((FEAT, TP * HID), BF16),
            pltpu.VMEM((CHUNKS, ROWS, TOK), BF16),
            pltpu.VMEM((3, CHUNKS, TOK, ROWS), BF16),
            pltpu.VMEM((3, TOK, FEAT), BF16),
            pltpu.VMEM((4, CHUNKS, ROWS, FEAT), BF16),
            pltpu.VMEM((TP, CHUNKS, ROWS, FEAT), BF16),
            pltpu.VMEM((ROWS, HID), F32),
            pltpu.VMEM((ROWS, HID), F32),
            pltpu.VMEM((TP, CHUNKS, ROWS, HID), BF16),
            pltpu.VMEM((CHUNKS, ROWS, FEAT), BF16),
            pltpu.VMEM((CHUNKS, ROWS, FEAT), BF16),
            pltpu.VMEM((TOK, FEAT), F32),
            dma((3,)),
            dma((3,)),
            dma((3,)),
            dma((4, CHUNKS)),
            dma((TP, CHUNKS)),
            dma((4, CHUNKS)),
            dma((8, CHUNKS)),
            dma((TP, CHUNKS)),
            dma((2, CHUNKS)),
            dma((CHUNKS,)),
            dma((CHUNKS,)),
        ],
        compiler_params=pltpu.CompilerParams(
            collective_id=0, has_side_effects=True, vmem_limit_bytes=58 * 2**20
        ),
        cost_estimate=pl.CostEstimate(flops=12 * 10**9, bytes_accessed=12 * 10**6, transcendentals=1024 * 256),
    )(
        indices, scores, tokens,
        gate_weight.reshape(TP, FEAT, HID), up_weight.reshape(TP, FEAT, HID), down_weight[0],
    )


def solution(mesh):
    placed = (
        P("ep", "tp"),
        P("ep", None),
        P("ep", None),
        P("ep", None, "tp"),
        P("ep", None, "tp"),
        P("ep", "tp", None),
    )
    return jax.shard_map(
        local, mesh=mesh, in_specs=placed, out_specs=P("ep", "tp"), check_vma=False
    )
```

```python
import functools

import jax
import jax.numpy as jnp
from jax import lax
from jax.experimental import pallas as pl
from jax.experimental.pallas import tpu as pltpu
from jax.sharding import PartitionSpec as P

MESH = pl.DeviceIdType.MESH
BF16 = jnp.bfloat16
F32 = jnp.float32
TP = 8
CAP = 32
TOK = 128
FEAT = 896
HID = 256
TOPK = 8
PEERS = 32
CHUNKS = 8
BLOCKS = PEERS // CHUNKS
ROWS = BLOCKS * CAP
HALF = TOK // 2
DIRECT = (0, 2, 6, 4, 1, 7)
TOKEN_SHIFTS = (2, 6, 4, 1, 7)
PLUS = (6, 7)
MINUS = (6, 7)
AHEAD_OWN = 4
AHEAD = 2
AHEAD_LATE = 1
AHEAD_HAND = 0
LAG_HALF = 1
LAG_HOP2 = 1
LAG_HOP3 = 1
LAG_DOWN = 2
LAG_MIX = 3


def among(c, chunks):
    yes = c < 0
    for v in chunks:
        yes = jnp.logical_or(yes, c == v)
    return yes


def dot(a, b):
    return jnp.dot(a, b, preferred_element_type=F32)


def kernel(
    idx_ref, score_ref, tok_in, gate_hbm, up_hbm, down_hbm,
    out_ref,
    w_gate, w_up, w_down, pick, route, tok, outgoing, x, acc_gate, acc_up, hid, res, ret, mix,
    w_sem, tok_send, tok_recv, half_send, half_arrive, x_send, x_recv, fwd_send, hid_send, hid_recv, half_recv, ret_send, ret_recv,
):
    z = lax.axis_index("tp")
    e = lax.axis_index("ep")
    ex, ey, ec = lax.div(e, 8), lax.rem(lax.div(e, 2), 4), lax.rem(e, 2)

    def plane(shift):
        return lax.rem(z + shift, TP)

    def peer(c, b, sign):
        k = c * BLOCKS + b
        far, core, pair = 2 * (b % 2), lax.rem(lax.div(k, 2), 2), lax.div(k, 4)
        px = lax.rem(ex + sign * (lax.div(pair, 4) + far) + 8, 4)
        py = lax.rem(ey + sign * (lax.rem(pair, 4) + far) + 8, 4)
        pc = lax.rem(ec + core, 2)
        return (z, (px * 4 + py) * 2 + pc)

    barrier = pltpu.get_barrier_semaphore()

    def greet(c, _):
        for b in range(BLOCKS):
            if b == 0:
                @pl.when(c > 0)
                def _():
                    pl.semaphore_signal(barrier, inc=1, device_id=peer(c, b, 1), device_id_type=MESH)
            else:
                pl.semaphore_signal(barrier, inc=1, device_id=peer(c, b, 1), device_id_type=MESH)
        return 0

    lax.fori_loop(0, CHUNKS, greet, 0)
    for shift in (1, 7, 2, 6, 4):
        pl.semaphore_signal(barrier, inc=1, device_id=(plane(shift), e), device_id_type=MESH)

    weights = [
        pltpu.make_async_copy(gate_hbm, w_gate, w_sem.at[0]),
        pltpu.make_async_copy(up_hbm, w_up, w_sem.at[1]),
        pltpu.make_async_copy(down_hbm, w_down, w_sem.at[2]),
    ]
    for copy in weights:
        copy.start()

    lane = lax.broadcasted_iota(jnp.int32, (TOK, 128), 1)
    row = lax.broadcasted_iota(jnp.int32, (TOK, 128), 0)
    offset = lax.broadcasted_iota(jnp.int32, (PEERS, TOK), 0)
    far = 2 * (offset & 1)
    at_x = (ex + (offset >> 4) + far) & 3
    at_y = (ey + ((offset >> 2) & 3) + far) & 3
    at_c = (ec + (offset >> 1)) & 1
    expert = (at_x * 4 + at_y) * 2 + at_c
    scores = score_ref[...]
    share = 2.5 * scores / jnp.sum(scores, axis=0, keepdims=True)
    chosen = jnp.zeros((PEERS, TOK), F32)
    weight = jnp.zeros((PEERS, TOK), F32)
    for j in range(TOPK):
        hit = idx_ref[j : j + 1, :] == expert
        chosen = jnp.where(hit, 1.0, chosen)
        weight = jnp.where(hit, share[j : j + 1, :], weight)
    before = jnp.where(row < lane, 1.0, 0.0).astype(BF16)
    slot_t = jnp.where(chosen > 0.5, dot(chosen.astype(BF16), before), -1.0)
    place = lax.broadcasted_iota(jnp.int32, (CAP, TOK), 0).astype(F32)
    for k in range(PEERS):
        pick[k // BLOCKS, (k % BLOCKS) * CAP : (k % BLOCKS + 1) * CAP, :] = jnp.where(
            slot_t[k : k + 1, :] == place, 1.0, 0.0
        ).astype(BF16)

    pl.semaphore_wait(barrier, PEERS - 1 + 5)

    def token_copy(n):
        shift = TOKEN_SHIFTS[n]
        return pltpu.make_async_remote_copy(
            src_ref=tok_in, dst_ref=tok.at[n], send_sem=tok_send.at[n], recv_sem=tok_recv.at[n],
            device_id=(plane(TP - shift), e), device_id_type=MESH,
        )

    def relay(n):
        shift = TOKEN_SHIFTS[n]
        rows = pl.ds(n * HALF, HALF)
        return pltpu.make_async_remote_copy(
            src_ref=tok.at[n, rows], dst_ref=tok.at[2, rows], send_sem=half_send.at[n], recv_sem=half_arrive.at[n],
            device_id=(plane(TP - shift), e), device_id_type=MESH,
        )

    for n in (0, 1):
        token_copy(n).start()

    def dispatch(n, c):
        d = DIRECT[n]
        source = tok_in[...] if n == 0 else tok[n - 1]
        outgoing[n, c] = dot(pick[c], source).astype(BF16)
        for b in range(BLOCKS):
            rows = pl.ds(b * CAP, CAP)

            def remote():
                pltpu.make_async_remote_copy(
                    src_ref=outgoing.at[n, c, rows], dst_ref=x.at[d, c, rows],
                    send_sem=x_send.at[n, c], recv_sem=x_recv.at[d, c],
                    device_id=peer(c, b, 1), device_id_type=MESH,
                ).start()

            def own():
                pltpu.make_async_copy(outgoing.at[n, c, rows], x.at[d, c, rows], x_recv.at[d, c]).start()

            if b == 0:
                pl.when(c > 0)(remote)
                pl.when(c == 0)(own)
            else:
                remote()

    def wait(ref, sem):
        pltpu.make_async_copy(ref, ref, sem).wait()

    def arrived(d, c):
        wait(x.at[d, c], x_recv.at[d, c])

    def hand_on(d, c, step, n):
        there = (d - step) % TP
        pltpu.make_async_remote_copy(
            src_ref=x.at[d, c], dst_ref=x.at[there, c],
            send_sem=fwd_send.at[n, c], recv_sem=x_recv.at[there, c],
            device_id=(plane(step % TP), e), device_id_type=MESH,
        ).start()

    def gate_up(c, offsets, gate, up):
        for d in offsets:
            rows = x[d, c]
            at = plane(d)
            g, u = dot(rows, w_gate[at]), dot(rows, w_up[at])
            gate = g if gate is None else gate + g
            up = u if up is None else up + u
        return gate, up

    def hid_copy(src, c, shift, n, half=None):
        rows = pl.ds(0, ROWS) if half is None else pl.ds(half * (ROWS // 2), ROWS // 2)
        recv = half_recv.at[half, c] if half is not None else hid_recv.at[src, c]
        pltpu.make_async_remote_copy(
            src_ref=hid.at[src, c, rows], dst_ref=hid.at[src, c, rows],
            send_sem=hid_send.at[n, c], recv_sem=recv,
            device_id=(plane(shift), e), device_id_type=MESH,
        ).start()

    def hid_wait(src, c):
        wait(hid.at[src, c], hid_recv.at[src, c])

    def first_half(c):
        gate, up = gate_up(c, (0, 2, 6), None, None)
        acc_gate[lax.rem(c, 4)] = gate
        acc_up[lax.rem(c, 4)] = up

    def second_half(c):
        for d in (4, 1, 7, 3, 5):
            arrived(d, c)
        gate, up = gate_up(c, (4, 1, 7, 3, 5), acc_gate[lax.rem(c, 4)], acc_up[lax.rem(c, 4)])
        hid[z, c] = (gate / (1.0 + jnp.exp(-gate)) * up).astype(BF16)
        hid_copy(z, c, 1, 0)
        hid_copy(z, c, 7, 1)

    def second_hop(c):
        hid_wait(plane(7), c)
        hid_copy(plane(7), c, 1, 2)
        hid_wait(plane(1), c)
        hid_copy(plane(1), c, 7, 3)

    def third_hop(c):
        hid_wait(plane(6), c)
        hid_copy(plane(6), c, 1, 4)
        hid_copy(plane(6), c, 2, 5, half=0)
        hid_wait(plane(2), c)
        hid_copy(plane(2), c, 7, 6)
        hid_copy(plane(2), c, 6, 7, half=1)

    def ret_block(c, b):
        rows = pl.ds(b * CAP, CAP)

        def remote():
            pltpu.make_async_remote_copy(
                src_ref=res.at[c, rows], dst_ref=ret.at[c, rows],
                send_sem=ret_send.at[c], recv_sem=ret_recv.at[c],
                device_id=peer(c, b, -1), device_id_type=MESH,
            ).start()

        def own():
            pltpu.make_async_copy(res.at[c, rows], ret.at[c, rows], ret_recv.at[c]).start()

        if b == 0:
            pl.when(c > 0)(remote)
            pl.when(c == 0)(own)
        else:
            remote()

    def down(c):
        hid_wait(plane(5), c)
        hid_wait(plane(3), c)
        for half in range(2):
            rows = pl.ds(half * (ROWS // 2), ROWS // 2)
            wait(hid.at[plane(4), c, rows], half_recv.at[half, c])
        total = None
        for s in range(TP):
            part = lax.dot_general(
                hid[s, c], w_down[:, s * HID : (s + 1) * HID], (((1,), (1,)), ((), ())),
                preferred_element_type=F32,
            )
            total = part if total is None else total + part
        res[c] = total.astype(BF16)
        for b in range(BLOCKS):
            ret_block(c, b)

    def combine(c):
        wait(ret.at[c], ret_recv.at[c])
        rows = ret[c]
        mix[...] += dot(route[0, c], rows) + dot(route[1, c], rows) + dot(route[2, c], rows)

    for c in range(AHEAD_OWN):
        dispatch(0, c)

    pad = TOK - PEERS
    slot = jnp.concatenate([slot_t, jnp.full((pad, TOK), -1.0, F32)], axis=0).T
    weight = jnp.concatenate([weight, jnp.zeros((pad, TOK), F32)], axis=0).T
    high = weight.astype(BF16)
    rest = weight - high.astype(F32)
    middle = rest.astype(BF16)
    low = (rest - middle.astype(F32)).astype(BF16)
    slot_b = slot.astype(BF16)

    def spread(c, _):
        to_row = lax.broadcasted_iota(jnp.int32, (TOK, ROWS), 0)
        to_lane = lax.broadcasted_iota(jnp.int32, (TOK, ROWS), 1)
        take = jnp.where(to_row == c * BLOCKS + (to_lane >> 5), 1.0, 0.0).astype(BF16)
        here = dot(slot_b, take) == (to_lane & (CAP - 1)).astype(F32)
        for n, part in enumerate((high, middle, low)):
            route[n, c] = jnp.where(here, dot(part, take), 0.0).astype(BF16)
        return 0

    lax.fori_loop(0, CHUNKS, spread, 0)
    mix[...] = jnp.zeros_like(mix)

    for n in (0, 1):
        wait(tok.at[n], tok_recv.at[n])
        relay(n).start()
        if (PLUS, MINUS)[n]:
            token_copy(n + 3).start()
        if n == 1:
            for c in range(AHEAD):
                dispatch(1, c)
                dispatch(2, c)
    for copy in weights:
        copy.wait()

    def own_slice(c):
        arrived(0, c)

        @pl.when(jnp.logical_not(among(c, MINUS)))
        def _():
            hand_on(0, c, 1, 0)

        @pl.when(jnp.logical_not(among(c, PLUS)))
        def _():
            hand_on(0, c, -1, 1)

    def dispatch_late(c):
        @pl.when(c == 0)
        def _():
            for n in (0, 1):
                half = tok.at[2, pl.ds(n * HALF, HALF)]
                wait(half, half_arrive.at[n])

        dispatch(3, c)
        for n, chunks in ((4, PLUS), (5, MINUS)):
            if not chunks:
                continue

            @pl.when(c == chunks[0])
            def _():
                wait(tok.at[n - 1], tok_recv.at[n - 1])

            @pl.when(among(c, chunks))
            def _():
                dispatch(n, c)

    for c in range(AHEAD_HAND):
        own_slice(c)

    def step(j, _):
        def at(lag, do):
            c = j - lag
            pl.when(jnp.logical_and(c >= 0, c < CHUNKS))(lambda: do(c))

        def other_slices(c):
            arrived(2, c)
            hand_on(2, c, -1, 2)
            arrived(6, c)
            hand_on(6, c, 1, 3)

        def dispatch_ahead(c):
            dispatch(1, c)
            dispatch(2, c)

        at(LAG_HALF, second_half)
        at(-AHEAD_HAND, own_slice)
        for early in range(AHEAD_LATE):
            pl.when(j == 0)(functools.partial(dispatch_late, early))
        at(-AHEAD_LATE, dispatch_late)
        at(LAG_HOP2, second_hop)
        at(-AHEAD_OWN, lambda c: dispatch(0, c))
        at(-AHEAD, dispatch_ahead)
        at(0, other_slices)
        at(LAG_DOWN, down)
        at(0, first_half)
        at(LAG_HOP3, third_hop)
        at(LAG_MIX, combine)
        return 0

    lax.fori_loop(0, CHUNKS + LAG_MIX, step, 0)

    out_ref[...] = mix[...].astype(BF16)

    for n in (0, 1) + ((3,) if PLUS else ()) + ((4,) if MINUS else ()):
        wait(tok_in, tok_send.at[n])
    for n in (0, 1):
        half = tok.at[n, pl.ds(n * HALF, HALF)]
        wait(half, half_send.at[n])

    def drain(c, _):
        for n in range(4):
            @pl.when(c > 0)
            def _():
                wait(outgoing.at[n, c], x_send.at[n, c])

            @pl.when(c == 0)
            def _():
                part = outgoing.at[n, c, pl.ds(CAP, ROWS - CAP)]
                wait(part, x_send.at[n, c])

        for n, other, chunks in ((4, 1, PLUS), (5, 0, MINUS)):
            @pl.when(among(c, chunks))
            def _():
                wait(outgoing.at[n, c], x_send.at[n, c])

            @pl.when(jnp.logical_not(among(c, chunks)))
            def _():
                wait(x.at[0, c], fwd_send.at[other, c])

        for n in range(2, 4):
            wait(x.at[0, c], fwd_send.at[n, c])
        for n in range(8):
            if n in (5, 7):
                half = hid.at[0, c, pl.ds(0, ROWS // 2)]
                wait(half, hid_send.at[n, c])
            else:
                wait(hid.at[0, c], hid_send.at[n, c])

        @pl.when(c > 0)
        def _():
            wait(res.at[c], ret_send.at[c])

        @pl.when(c == 0)
        def _():
            part = res.at[c, pl.ds(CAP, ROWS - CAP)]
            wait(part, ret_send.at[c])

        return 0

    lax.fori_loop(0, CHUNKS, drain, 0)


def local(tokens, indices, scores, gate_weight, up_weight, down_weight):
    vmem = pl.BlockSpec(memory_space=pltpu.VMEM)
    anywhere = pl.BlockSpec(memory_space=pl.ANY)
    dma = pltpu.SemaphoreType.DMA
    return pl.pallas_call(
        kernel,
        out_shape=jax.ShapeDtypeStruct((TOK, FEAT), BF16),
        in_specs=[vmem, vmem, vmem, anywhere, anywhere, anywhere],
        out_specs=vmem,
        scratch_shapes=[
            pltpu.VMEM((TP, FEAT, HID), BF16),
            pltpu.VMEM((TP, FEAT, HID), BF16),
            pltpu.VMEM((FEAT, TP * HID), BF16),
            pltpu.VMEM((CHUNKS, ROWS, TOK), BF16),
            pltpu.VMEM((3, CHUNKS, TOK, ROWS), BF16),
            pltpu.VMEM((5, TOK, FEAT), BF16),
            pltpu.VMEM((6, CHUNKS, ROWS, FEAT), BF16),
            pltpu.VMEM((TP, CHUNKS, ROWS, FEAT), BF16),
            pltpu.VMEM((4, ROWS, HID), F32),
            pltpu.VMEM((4, ROWS, HID), F32),
            pltpu.VMEM((TP, CHUNKS, ROWS, HID), BF16),
            pltpu.VMEM((CHUNKS, ROWS, FEAT), BF16),
            pltpu.VMEM((CHUNKS, ROWS, FEAT), BF16),
            pltpu.VMEM((TOK, FEAT), F32),
            dma((3,)),
            dma((5,)),
            dma((5,)),
            dma((2,)),
            dma((2,)),
            dma((6, CHUNKS)),
            dma((TP, CHUNKS)),
            dma((4, CHUNKS)),
            dma((8, CHUNKS)),
            dma((TP, CHUNKS)),
            dma((2, CHUNKS)),
            dma((CHUNKS,)),
            dma((CHUNKS,)),
        ],
        compiler_params=pltpu.CompilerParams(
            collective_id=0, has_side_effects=True, vmem_limit_bytes=58 * 2**20
        ),
        cost_estimate=pl.CostEstimate(flops=12 * 10**9, bytes_accessed=12 * 10**6, transcendentals=1024 * 256),
    )(
        indices.T, scores.T, tokens,
        gate_weight.reshape(TP, FEAT, HID), up_weight.reshape(TP, FEAT, HID), down_weight[0],
    )


def solution(mesh):
    placed = (
        P("ep", "tp"),
        P("ep", None),
        P("ep", None),
        P("ep", None, "tp"),
        P("ep", None, "tp"),
        P("ep", "tp", None),
    )
    return jax.shard_map(
        local, mesh=mesh, in_specs=placed, out_specs=P("ep", "tp"), check_vma=False
    )
```

```python
import functools

import jax
import jax.numpy as jnp
from jax import lax
from jax.experimental import pallas as pl
from jax.experimental.pallas import tpu as pltpu
from jax.sharding import PartitionSpec as P

MESH = pl.DeviceIdType.MESH
BF16 = jnp.bfloat16
F32 = jnp.float32
TP = 8
CAP = 32
TOK = 128
FEAT = 896
HID = 256
TOPK = 8
PEERS = 32
CHUNKS = 8
BLOCKS = PEERS // CHUNKS
ROWS = BLOCKS * CAP
HALF = TOK // 2
DIRECT = (0, 2, 6, 4, 1, 7)
TOKEN_SHIFTS = (2, 6, 4, 1, 7)
PLUS = (6, 7)
MINUS = (6, 7)
AHEAD_OWN = 4
AHEAD = 2
AHEAD_LATE = 1
AHEAD_HAND = 0
RAMP = 1
LAG_HALF = 1
LAG_HOP2 = 1
LAG_HOP3 = 1
LAG_HOP4 = 2
LAG_DOWN = 2
LAG_MIX = 3


def among(c, chunks):
    yes = c < 0
    for v in chunks:
        yes = jnp.logical_or(yes, c == v)
    return yes


def dot(a, b):
    return jnp.dot(a, b, preferred_element_type=F32)


def kernel(
    idx_ref, score_ref, tok_in, gate_hbm, up_hbm, down_hbm,
    out_ref,
    w_gate, w_up, w_down, pick, route, tok, outgoing, x, acc_gate, acc_up, hid, res, ret, mix,
    w_sem, tok_send, tok_recv, half_send, half_arrive, x_send, x_recv, fwd_send, hid_send, hid_recv, half_recv, ret_send, ret_recv,
):
    z = lax.axis_index("tp")
    e = lax.axis_index("ep")
    ex, ey, ec = lax.div(e, 8), lax.rem(lax.div(e, 2), 4), lax.rem(e, 2)

    def plane(shift):
        return lax.rem(z + shift, TP)

    def peer(c, b, sign):
        k = c * BLOCKS + b
        far, core, pair = 2 * (b % 2), lax.rem(lax.div(k, 2), 2), lax.div(k, 4)
        px = lax.rem(ex + sign * (lax.div(pair, 4) + far) + 8, 4)
        py = lax.rem(ey + sign * (lax.rem(pair, 4) + far) + 8, 4)
        pc = lax.rem(ec + core, 2)
        return (z, (px * 4 + py) * 2 + pc)

    barrier = pltpu.get_barrier_semaphore()

    def greet(c, _):
        for b in range(BLOCKS):
            if b == 0:
                @pl.when(c > 0)
                def _():
                    pl.semaphore_signal(barrier, inc=1, device_id=peer(c, b, 1), device_id_type=MESH)
            else:
                pl.semaphore_signal(barrier, inc=1, device_id=peer(c, b, 1), device_id_type=MESH)
        return 0

    lax.fori_loop(0, CHUNKS, greet, 0)
    for shift in (1, 7, 2, 6, 4):
        pl.semaphore_signal(barrier, inc=1, device_id=(plane(shift), e), device_id_type=MESH)

    weights = [
        pltpu.make_async_copy(gate_hbm, w_gate, w_sem.at[0]),
        pltpu.make_async_copy(up_hbm, w_up, w_sem.at[1]),
        pltpu.make_async_copy(down_hbm, w_down, w_sem.at[2]),
    ]
    for copy in weights:
        copy.start()

    lane = lax.broadcasted_iota(jnp.int32, (TOK, 128), 1)
    row = lax.broadcasted_iota(jnp.int32, (TOK, 128), 0)
    offset = lax.broadcasted_iota(jnp.int32, (PEERS, TOK), 0)
    far = 2 * (offset & 1)
    at_x = (ex + (offset >> 4) + far) & 3
    at_y = (ey + ((offset >> 2) & 3) + far) & 3
    at_c = (ec + (offset >> 1)) & 1
    expert = (at_x * 4 + at_y) * 2 + at_c
    scores = score_ref[...]
    share = 2.5 * scores / jnp.sum(scores, axis=0, keepdims=True)
    chosen = jnp.zeros((PEERS, TOK), F32)
    weight = jnp.zeros((PEERS, TOK), F32)
    for j in range(TOPK):
        hit = idx_ref[j : j + 1, :] == expert
        chosen = jnp.where(hit, 1.0, chosen)
        weight = jnp.where(hit, share[j : j + 1, :], weight)
    before = jnp.where(row < lane, 1.0, 0.0).astype(BF16)
    slot_t = jnp.where(chosen > 0.5, dot(chosen.astype(BF16), before), -1.0)
    place = lax.broadcasted_iota(jnp.int32, (CAP, TOK), 0).astype(F32)
    for k in range(PEERS):
        pick[k // BLOCKS, (k % BLOCKS) * CAP : (k % BLOCKS + 1) * CAP, :] = jnp.where(
            slot_t[k : k + 1, :] == place, 1.0, 0.0
        ).astype(BF16)

    pl.semaphore_wait(barrier, PEERS - 1 + 5)

    def token_copy(n):
        shift = TOKEN_SHIFTS[n]
        return pltpu.make_async_remote_copy(
            src_ref=tok_in, dst_ref=tok.at[n], send_sem=tok_send.at[n], recv_sem=tok_recv.at[n],
            device_id=(plane(TP - shift), e), device_id_type=MESH,
        )

    def relay(n):
        shift = TOKEN_SHIFTS[n]
        rows = pl.ds(n * HALF, HALF)
        return pltpu.make_async_remote_copy(
            src_ref=tok.at[n, rows], dst_ref=tok.at[2, rows], send_sem=half_send.at[n], recv_sem=half_arrive.at[n],
            device_id=(plane(TP - shift), e), device_id_type=MESH,
        )

    for n in (0, 1):
        token_copy(n).start()

    def dispatch(n, c):
        d = DIRECT[n]
        source = tok_in[...] if n == 0 else tok[n - 1]
        outgoing[n, c] = dot(pick[c], source).astype(BF16)
        for b in range(BLOCKS):
            rows = pl.ds(b * CAP, CAP)

            def remote():
                pltpu.make_async_remote_copy(
                    src_ref=outgoing.at[n, c, rows], dst_ref=x.at[d, c, rows],
                    send_sem=x_send.at[n, c], recv_sem=x_recv.at[d, c],
                    device_id=peer(c, b, 1), device_id_type=MESH,
                ).start()

            def own():
                pltpu.make_async_copy(outgoing.at[n, c, rows], x.at[d, c, rows], x_recv.at[d, c]).start()

            if b == 0:
                pl.when(c > 0)(remote)
                pl.when(c == 0)(own)
            else:
                remote()

    def wait(ref, sem):
        pltpu.make_async_copy(ref, ref, sem).wait()

    def arrived(d, c):
        wait(x.at[d, c], x_recv.at[d, c])

    def hand_on(d, c, step, n):
        there = (d - step) % TP
        pltpu.make_async_remote_copy(
            src_ref=x.at[d, c], dst_ref=x.at[there, c],
            send_sem=fwd_send.at[n, c], recv_sem=x_recv.at[there, c],
            device_id=(plane(step % TP), e), device_id_type=MESH,
        ).start()

    def gate_up(c, offsets, gate, up):
        for d in offsets:
            rows = x[d, c]
            at = plane(d)
            g, u = dot(rows, w_gate[at]), dot(rows, w_up[at])
            gate = g if gate is None else gate + g
            up = u if up is None else up + u
        return gate, up

    def hid_copy(src, c, shift, n, half=None):
        rows = pl.ds(0, ROWS) if half is None else pl.ds(half * (ROWS // 2), ROWS // 2)
        recv = half_recv.at[half, c] if half is not None else hid_recv.at[src, c]
        pltpu.make_async_remote_copy(
            src_ref=hid.at[src, c, rows], dst_ref=hid.at[src, c, rows],
            send_sem=hid_send.at[n, c], recv_sem=recv,
            device_id=(plane(shift), e), device_id_type=MESH,
        ).start()

    def hid_wait(src, c):
        wait(hid.at[src, c], hid_recv.at[src, c])

    def first_half(c):
        gate, up = gate_up(c, (0, 2, 6), None, None)
        acc_gate[lax.rem(c, 4)] = gate
        acc_up[lax.rem(c, 4)] = up

    def second_half(c):
        for d in (4, 1, 7, 3, 5):
            arrived(d, c)
        gate, up = gate_up(c, (4, 1, 7, 3, 5), acc_gate[lax.rem(c, 4)], acc_up[lax.rem(c, 4)])
        hid[z, c] = (gate / (1.0 + jnp.exp(-gate)) * up).astype(BF16)
        hid_copy(z, c, 1, 0)
        hid_copy(z, c, 7, 1)

    def second_hop(c):
        hid_wait(plane(7), c)
        hid_copy(plane(7), c, 1, 2)
        hid_wait(plane(1), c)
        hid_copy(plane(1), c, 7, 3)

    def third_hop(c):
        last = c == CHUNKS - 1
        hid_wait(plane(6), c)
        hid_copy(plane(6), c, 1, 4)
        pl.when(last)(lambda: hid_copy(plane(6), c, 2, 5, half=0))
        hid_wait(plane(2), c)
        hid_copy(plane(2), c, 7, 6)
        pl.when(last)(lambda: hid_copy(plane(2), c, 6, 7, half=1))

    def fourth_hop(c):
        last = c == CHUNKS - 1
        hid_wait(plane(5), c)
        pl.when(jnp.logical_not(last))(lambda: hid_copy(plane(5), c, 1, 5, half=0))
        hid_wait(plane(3), c)
        pl.when(jnp.logical_not(last))(lambda: hid_copy(plane(3), c, 7, 7, half=1))

    def ret_block(c, b):
        rows = pl.ds(b * CAP, CAP)

        def remote():
            pltpu.make_async_remote_copy(
                src_ref=res.at[c, rows], dst_ref=ret.at[c, rows],
                send_sem=ret_send.at[c], recv_sem=ret_recv.at[c],
                device_id=peer(c, b, -1), device_id_type=MESH,
            ).start()

        def own():
            pltpu.make_async_copy(res.at[c, rows], ret.at[c, rows], ret_recv.at[c]).start()

        if b == 0:
            pl.when(c > 0)(remote)
            pl.when(c == 0)(own)
        else:
            remote()

    def down(c):
        for half in range(2):
            rows = pl.ds(half * (ROWS // 2), ROWS // 2)
            wait(hid.at[plane(4), c, rows], half_recv.at[half, c])
        total = None
        for s in range(TP):
            part = lax.dot_general(
                hid[s, c], w_down[:, s * HID : (s + 1) * HID], (((1,), (1,)), ((), ())),
                preferred_element_type=F32,
            )
            total = part if total is None else total + part
        res[c] = total.astype(BF16)
        for b in range(BLOCKS):
            ret_block(c, b)

    def combine(c):
        wait(ret.at[c], ret_recv.at[c])
        rows = ret[c]
        mix[...] += dot(route[0, c], rows) + dot(route[1, c], rows) + dot(route[2, c], rows)

    for c in range(AHEAD_OWN):
        dispatch(0, c)

    pad = TOK - PEERS
    slot = jnp.concatenate([slot_t, jnp.full((pad, TOK), -1.0, F32)], axis=0).T
    weight = jnp.concatenate([weight, jnp.zeros((pad, TOK), F32)], axis=0).T
    high = weight.astype(BF16)
    rest = weight - high.astype(F32)
    middle = rest.astype(BF16)
    low = (rest - middle.astype(F32)).astype(BF16)
    slot_b = slot.astype(BF16)

    def spread(c, _):
        to_row = lax.broadcasted_iota(jnp.int32, (TOK, ROWS), 0)
        to_lane = lax.broadcasted_iota(jnp.int32, (TOK, ROWS), 1)
        take = jnp.where(to_row == c * BLOCKS + (to_lane >> 5), 1.0, 0.0).astype(BF16)
        here = dot(slot_b, take) == (to_lane & (CAP - 1)).astype(F32)
        for n, part in enumerate((high, middle, low)):
            route[n, c] = jnp.where(here, dot(part, take), 0.0).astype(BF16)
        return 0

    lax.fori_loop(0, CHUNKS, spread, 0)
    mix[...] = jnp.zeros_like(mix)

    for n in (0, 1):
        wait(tok.at[n], tok_recv.at[n])
        relay(n).start()
        if (PLUS, MINUS)[n]:
            token_copy(n + 3).start()
        if n == 1:
            for c in range(AHEAD):
                dispatch(1, c)
                dispatch(2, c)
    for copy in weights:
        copy.wait()

    def own_slice(c):
        arrived(0, c)

        @pl.when(jnp.logical_not(among(c, MINUS)))
        def _():
            hand_on(0, c, 1, 0)

        @pl.when(jnp.logical_not(among(c, PLUS)))
        def _():
            hand_on(0, c, -1, 1)

    def dispatch_late(c):
        @pl.when(c == 0)
        def _():
            for n in (0, 1):
                half = tok.at[2, pl.ds(n * HALF, HALF)]
                wait(half, half_arrive.at[n])

        dispatch(3, c)
        for n, chunks in ((4, PLUS), (5, MINUS)):
            if not chunks:
                continue

            @pl.when(c == chunks[0])
            def _():
                wait(tok.at[n - 1], tok_recv.at[n - 1])

            @pl.when(among(c, chunks))
            def _():
                dispatch(n, c)

    for c in range(AHEAD_HAND):
        own_slice(c)

    def step(j, _):
        def ahead(lead, do):
            first = jnp.where(j > RAMP, j + lead + 1, j + lead)
            end = jnp.where(j >= RAMP, j + lead + 2, j + lead + 1)

            def one(c, _):
                do(c)
                return 0

            lax.fori_loop(jnp.minimum(first, CHUNKS), jnp.minimum(end, CHUNKS), one, 0)

        def at(lag, do):
            c = j - lag
            pl.when(jnp.logical_and(c >= 0, c < CHUNKS))(lambda: do(c))

        def other_slices(c):
            arrived(2, c)
            hand_on(2, c, -1, 2)
            arrived(6, c)
            hand_on(6, c, 1, 3)

        def dispatch_ahead(c):
            dispatch(1, c)
            dispatch(2, c)

        at(LAG_HALF, second_half)
        at(-AHEAD_HAND, own_slice)
        for early in range(AHEAD_LATE):
            pl.when(j == 0)(functools.partial(dispatch_late, early))
        at(-AHEAD_LATE, dispatch_late)
        at(LAG_HOP4, fourth_hop)
        at(LAG_HOP2, second_hop)
        ahead(AHEAD_OWN, lambda c: dispatch(0, c))
        ahead(AHEAD, dispatch_ahead)
        at(0, other_slices)
        at(LAG_DOWN, down)
        at(0, first_half)
        at(LAG_HOP3, third_hop)
        at(LAG_MIX, combine)
        return 0

    lax.fori_loop(0, CHUNKS + LAG_MIX, step, 0)

    out_ref[...] = mix[...].astype(BF16)

    for n in (0, 1) + ((3,) if PLUS else ()) + ((4,) if MINUS else ()):
        wait(tok_in, tok_send.at[n])
    for n in (0, 1):
        half = tok.at[n, pl.ds(n * HALF, HALF)]
        wait(half, half_send.at[n])

    def drain(c, _):
        for n in range(4):
            @pl.when(c > 0)
            def _():
                wait(outgoing.at[n, c], x_send.at[n, c])

            @pl.when(c == 0)
            def _():
                part = outgoing.at[n, c, pl.ds(CAP, ROWS - CAP)]
                wait(part, x_send.at[n, c])

        for n, other, chunks in ((4, 1, PLUS), (5, 0, MINUS)):
            @pl.when(among(c, chunks))
            def _():
                wait(outgoing.at[n, c], x_send.at[n, c])

            @pl.when(jnp.logical_not(among(c, chunks)))
            def _():
                wait(x.at[0, c], fwd_send.at[other, c])

        for n in range(2, 4):
            wait(x.at[0, c], fwd_send.at[n, c])
        for n in range(8):
            if n in (5, 7):
                half = hid.at[0, c, pl.ds(0, ROWS // 2)]
                wait(half, hid_send.at[n, c])
            else:
                wait(hid.at[0, c], hid_send.at[n, c])

        @pl.when(c > 0)
        def _():
            wait(res.at[c], ret_send.at[c])

        @pl.when(c == 0)
        def _():
            part = res.at[c, pl.ds(CAP, ROWS - CAP)]
            wait(part, ret_send.at[c])

        return 0

    lax.fori_loop(0, CHUNKS, drain, 0)


def local(tokens, indices, scores, gate_weight, up_weight, down_weight):
    vmem = pl.BlockSpec(memory_space=pltpu.VMEM)
    anywhere = pl.BlockSpec(memory_space=pl.ANY)
    dma = pltpu.SemaphoreType.DMA
    return pl.pallas_call(
        kernel,
        out_shape=jax.ShapeDtypeStruct((TOK, FEAT), BF16),
        in_specs=[vmem, vmem, vmem, anywhere, anywhere, anywhere],
        out_specs=vmem,
        scratch_shapes=[
            pltpu.VMEM((TP, FEAT, HID), BF16),
            pltpu.VMEM((TP, FEAT, HID), BF16),
            pltpu.VMEM((FEAT, TP * HID), BF16),
            pltpu.VMEM((CHUNKS, ROWS, TOK), BF16),
            pltpu.VMEM((3, CHUNKS, TOK, ROWS), BF16),
            pltpu.VMEM((5, TOK, FEAT), BF16),
            pltpu.VMEM((6, CHUNKS, ROWS, FEAT), BF16),
            pltpu.VMEM((TP, CHUNKS, ROWS, FEAT), BF16),
            pltpu.VMEM((4, ROWS, HID), F32),
            pltpu.VMEM((4, ROWS, HID), F32),
            pltpu.VMEM((TP, CHUNKS, ROWS, HID), BF16),
            pltpu.VMEM((CHUNKS, ROWS, FEAT), BF16),
            pltpu.VMEM((CHUNKS, ROWS, FEAT), BF16),
            pltpu.VMEM((TOK, FEAT), F32),
            dma((3,)),
            dma((5,)),
            dma((5,)),
            dma((2,)),
            dma((2,)),
            dma((6, CHUNKS)),
            dma((TP, CHUNKS)),
            dma((4, CHUNKS)),
            dma((8, CHUNKS)),
            dma((TP, CHUNKS)),
            dma((2, CHUNKS)),
            dma((CHUNKS,)),
            dma((CHUNKS,)),
        ],
        compiler_params=pltpu.CompilerParams(
            collective_id=0, has_side_effects=True, vmem_limit_bytes=58 * 2**20
        ),
        cost_estimate=pl.CostEstimate(flops=12 * 10**9, bytes_accessed=12 * 10**6, transcendentals=1024 * 256),
    )(
        indices.T, scores.T, tokens,
        gate_weight.reshape(TP, FEAT, HID), up_weight.reshape(TP, FEAT, HID), down_weight[0],
    )


def solution(mesh):
    placed = (
        P("ep", "tp"),
        P("ep", None),
        P("ep", None),
        P("ep", None, "tp"),
        P("ep", None, "tp"),
        P("ep", "tp", None),
    )
    return jax.shard_map(
        local, mesh=mesh, in_specs=placed, out_specs=P("ep", "tp"), check_vma=False
    )
```

```python
import functools

import jax
import jax.numpy as jnp
from jax import lax
from jax.experimental import pallas as pl
from jax.experimental.pallas import tpu as pltpu
from jax.sharding import PartitionSpec as P

MESH = pl.DeviceIdType.MESH
BF16 = jnp.bfloat16
F32 = jnp.float32
TP = 8
CAP = 32
TOK = 128
FEAT = 896
HID = 256
TOPK = 8
PEERS = 32
CHUNKS = 8
BLOCKS = PEERS // CHUNKS
ROWS = BLOCKS * CAP
HALF = TOK // 2
DIRECT = (0, 2, 6, 4, 1, 7)
TOKEN_SHIFTS = (2, 6, 4, 1, 7)
PLUS = (6, 7)
MINUS = (6, 7)
AHEAD_OWN = 4
AHEAD = 2
AHEAD_LATE = 1
AHEAD_HAND = 0
RAMP = 1
LAG_HALF = 1
LAG_HOP2 = 1
LAG_HOP3 = 1
LAG_HOP4 = 2
LAG_DOWN = 2
LAG_MIX = 3


def among(c, chunks):
    yes = c < 0
    for v in chunks:
        yes = jnp.logical_or(yes, c == v)
    return yes


def dot(a, b):
    return jnp.dot(a, b, preferred_element_type=F32)


def kernel(
    idx_ref, score_ref, tok_in, gate_hbm, up_hbm, down_hbm,
    out_ref,
    w_gate, w_up, w_down, pick, route, tok, outgoing, x, acc_gate, acc_up, hid, res, ret, mix,
    w_sem, tok_send, tok_recv, half_send, half_arrive, x_send, x_recv, fwd_send, hid_send, hid_recv, half_recv, ret_send, ret_recv,
):
    z = lax.axis_index("tp")
    e = lax.axis_index("ep")
    ex, ey, ec = lax.div(e, 8), lax.rem(lax.div(e, 2), 4), lax.rem(e, 2)

    def plane(shift):
        return lax.rem(z + shift, TP)

    def peer(c, b, sign):
        k = c * BLOCKS + b
        far, core, pair = 2 * (b % 2), lax.rem(lax.div(k, 2), 2), lax.div(k, 4)
        px = lax.rem(ex + sign * (lax.div(pair, 4) + far) + 8, 4)
        py = lax.rem(ey + sign * (lax.rem(pair, 4) + far) + 8, 4)
        pc = lax.rem(ec + core, 2)
        return (z, (px * 4 + py) * 2 + pc)

    barrier = pltpu.get_barrier_semaphore()

    def greet(c, _):
        for b in range(BLOCKS):
            if b == 0:
                @pl.when(c > 0)
                def _():
                    pl.semaphore_signal(barrier, inc=1, device_id=peer(c, b, 1), device_id_type=MESH)
            else:
                pl.semaphore_signal(barrier, inc=1, device_id=peer(c, b, 1), device_id_type=MESH)
        return 0

    lax.fori_loop(0, CHUNKS, greet, 0)
    for shift in (1, 7, 2, 6, 4):
        pl.semaphore_signal(barrier, inc=1, device_id=(plane(shift), e), device_id_type=MESH)

    weights = [
        pltpu.make_async_copy(gate_hbm, w_gate, w_sem.at[0]),
        pltpu.make_async_copy(up_hbm, w_up, w_sem.at[1]),
        pltpu.make_async_copy(down_hbm, w_down, w_sem.at[2]),
    ]
    for copy in weights:
        copy.start()

    lane = lax.broadcasted_iota(jnp.int32, (TOK, 128), 1)
    row = lax.broadcasted_iota(jnp.int32, (TOK, 128), 0)
    offset = lax.broadcasted_iota(jnp.int32, (PEERS, TOK), 0)
    far = 2 * (offset & 1)
    at_x = (ex + (offset >> 4) + far) & 3
    at_y = (ey + ((offset >> 2) & 3) + far) & 3
    at_c = (ec + (offset >> 1)) & 1
    expert = (at_x * 4 + at_y) * 2 + at_c
    scores = score_ref[...]
    share = 2.5 * scores / jnp.sum(scores, axis=0, keepdims=True)
    chosen = jnp.zeros((PEERS, TOK), F32)
    weight = jnp.zeros((PEERS, TOK), F32)
    for j in range(TOPK):
        hit = idx_ref[j : j + 1, :] == expert
        chosen = jnp.where(hit, 1.0, chosen)
        weight = jnp.where(hit, share[j : j + 1, :], weight)
    before = jnp.where(row < lane, 1.0, 0.0).astype(BF16)
    slot_t = jnp.where(chosen > 0.5, dot(chosen.astype(BF16), before), -1.0)
    place = lax.broadcasted_iota(jnp.int32, (CAP, TOK), 0).astype(F32)
    for k in range(PEERS):
        pick[k // BLOCKS, (k % BLOCKS) * CAP : (k % BLOCKS + 1) * CAP, :] = jnp.where(
            slot_t[k : k + 1, :] == place, 1.0, 0.0
        ).astype(BF16)

    pl.semaphore_wait(barrier, PEERS - 1 + 5)

    def token_copy(n):
        shift = TOKEN_SHIFTS[n]
        return pltpu.make_async_remote_copy(
            src_ref=tok_in, dst_ref=tok.at[n], send_sem=tok_send.at[n], recv_sem=tok_recv.at[n],
            device_id=(plane(TP - shift), e), device_id_type=MESH,
        )

    def relay(n):
        shift = TOKEN_SHIFTS[n]
        rows = pl.ds(n * HALF, HALF)
        return pltpu.make_async_remote_copy(
            src_ref=tok.at[n, rows], dst_ref=tok.at[2, rows], send_sem=half_send.at[n], recv_sem=half_arrive.at[n],
            device_id=(plane(TP - shift), e), device_id_type=MESH,
        )

    for n in (0, 1):
        token_copy(n).start()

    def dispatch(n, c):
        d = DIRECT[n]
        source = tok_in[...] if n == 0 else tok[n - 1]
        outgoing[n, c] = dot(pick[c], source).astype(BF16)
        for b in range(BLOCKS):
            rows = pl.ds(b * CAP, CAP)

            def remote():
                pltpu.make_async_remote_copy(
                    src_ref=outgoing.at[n, c, rows], dst_ref=x.at[d, c, rows],
                    send_sem=x_send.at[n, c], recv_sem=x_recv.at[d, c],
                    device_id=peer(c, b, 1), device_id_type=MESH,
                ).start()

            def own():
                pltpu.make_async_copy(outgoing.at[n, c, rows], x.at[d, c, rows], x_recv.at[d, c]).start()

            if b == 0:
                pl.when(c > 0)(remote)
                pl.when(c == 0)(own)
            else:
                remote()

    def wait(ref, sem):
        pltpu.make_async_copy(ref, ref, sem).wait()

    def arrived(d, c):
        wait(x.at[d, c], x_recv.at[d, c])

    def hand_on(d, c, step, n):
        there = (d - step) % TP
        pltpu.make_async_remote_copy(
            src_ref=x.at[d, c], dst_ref=x.at[there, c],
            send_sem=fwd_send.at[n, c], recv_sem=x_recv.at[there, c],
            device_id=(plane(step % TP), e), device_id_type=MESH,
        ).start()

    def gate_up(c, offsets, gate, up):
        for d in offsets:
            rows = x[d, c]
            at = plane(d)
            g, u = dot(rows, w_gate[at]), dot(rows, w_up[at])
            gate = g if gate is None else gate + g
            up = u if up is None else up + u
        return gate, up

    def hid_copy(src, c, shift, n, half=None):
        rows = pl.ds(0, ROWS) if half is None else pl.ds(half * (ROWS // 2), ROWS // 2)
        recv = half_recv.at[half, c] if half is not None else hid_recv.at[src, c]
        pltpu.make_async_remote_copy(
            src_ref=hid.at[src, c, rows], dst_ref=hid.at[src, c, rows],
            send_sem=hid_send.at[n, c], recv_sem=recv,
            device_id=(plane(shift), e), device_id_type=MESH,
        ).start()

    def hid_wait(src, c):
        wait(hid.at[src, c], hid_recv.at[src, c])

    def first_half(c):
        gate, up = gate_up(c, (0, 2, 6), None, None)
        acc_gate[lax.rem(c, 4)] = gate
        acc_up[lax.rem(c, 4)] = up

    def second_half(c):
        for d in (4, 1, 7, 3, 5):
            arrived(d, c)
        gate, up = gate_up(c, (4, 1, 7, 3, 5), acc_gate[lax.rem(c, 4)], acc_up[lax.rem(c, 4)])
        hid[z, c] = (gate / (1.0 + jnp.exp(-gate)) * up).astype(BF16)
        hid_copy(z, c, 1, 0)
        hid_copy(z, c, 7, 1)

    def second_hop(c):
        hid_wait(plane(7), c)
        hid_copy(plane(7), c, 1, 2)
        hid_wait(plane(1), c)
        hid_copy(plane(1), c, 7, 3)

    def third_hop(c):
        last = c == CHUNKS - 1
        hid_wait(plane(6), c)
        hid_copy(plane(6), c, 1, 4)
        pl.when(last)(lambda: hid_copy(plane(6), c, 2, 5, half=0))
        hid_wait(plane(2), c)
        hid_copy(plane(2), c, 7, 6)
        pl.when(last)(lambda: hid_copy(plane(2), c, 6, 7, half=1))

    def fourth_hop(c):
        last = c == CHUNKS - 1
        hid_wait(plane(5), c)
        pl.when(jnp.logical_not(last))(lambda: hid_copy(plane(5), c, 1, 5, half=0))
        hid_wait(plane(3), c)
        pl.when(jnp.logical_not(last))(lambda: hid_copy(plane(3), c, 7, 7, half=1))

    def ret_block(c, b):
        rows = pl.ds(b * CAP, CAP)

        def remote():
            pltpu.make_async_remote_copy(
                src_ref=res.at[c, rows], dst_ref=ret.at[c, rows],
                send_sem=ret_send.at[c], recv_sem=ret_recv.at[c],
                device_id=peer(c, b, -1), device_id_type=MESH,
            ).start()

        def own():
            pltpu.make_async_copy(res.at[c, rows], ret.at[c, rows], ret_recv.at[c]).start()

        if b == 0:
            pl.when(c > 0)(remote)
            pl.when(c == 0)(own)
        else:
            remote()

    def down(c):
        for half in range(2):
            rows = pl.ds(half * (ROWS // 2), ROWS // 2)
            wait(hid.at[plane(4), c, rows], half_recv.at[half, c])
        total = None
        for s in range(TP):
            part = lax.dot_general(
                hid[s, c], w_down[:, s * HID : (s + 1) * HID], (((1,), (1,)), ((), ())),
                preferred_element_type=F32,
            )
            total = part if total is None else total + part
        res[c] = total.astype(BF16)
        for b in range(BLOCKS):
            ret_block(c, b)

    def combine(c):
        wait(ret.at[c], ret_recv.at[c])
        rows = ret[c]
        mix[...] += dot(route[0, c], rows) + dot(route[1, c], rows) + dot(route[2, c], rows)

    for c in range(AHEAD_OWN):
        dispatch(0, c)

    pad = TOK - PEERS
    slot = jnp.concatenate([slot_t, jnp.full((pad, TOK), -1.0, F32)], axis=0).T
    weight = jnp.concatenate([weight, jnp.zeros((pad, TOK), F32)], axis=0).T
    high = weight.astype(BF16)
    rest = weight - high.astype(F32)
    middle = rest.astype(BF16)
    low = (rest - middle.astype(F32)).astype(BF16)
    slot_b = slot.astype(BF16)

    def spread(c, _):
        to_row = lax.broadcasted_iota(jnp.int32, (TOK, ROWS), 0)
        to_lane = lax.broadcasted_iota(jnp.int32, (TOK, ROWS), 1)
        take = jnp.where(to_row == c * BLOCKS + (to_lane >> 5), 1.0, 0.0).astype(BF16)
        here = dot(slot_b, take) == (to_lane & (CAP - 1)).astype(F32)
        for n, part in enumerate((high, middle, low)):
            route[n, c] = jnp.where(here, dot(part, take), 0.0).astype(BF16)
        return 0

    lax.fori_loop(0, CHUNKS, spread, 0)
    mix[...] = jnp.zeros_like(mix)

    for n in (0, 1):
        wait(tok.at[n], tok_recv.at[n])
        relay(n).start()
        if (PLUS, MINUS)[n]:
            token_copy(n + 3).start()
        if n == 1:
            for c in range(AHEAD):
                dispatch(1, c)
                dispatch(2, c)
    for copy in weights:
        copy.wait()

    def own_slice(c):
        arrived(0, c)

        @pl.when(jnp.logical_not(among(c, MINUS)))
        def _():
            hand_on(0, c, 1, 0)

        @pl.when(jnp.logical_not(among(c, PLUS)))
        def _():
            hand_on(0, c, -1, 1)

    def dispatch_late(c):
        @pl.when(c == 0)
        def _():
            for n in (0, 1):
                half = tok.at[2, pl.ds(n * HALF, HALF)]
                wait(half, half_arrive.at[n])

        dispatch(3, c)
        for n, chunks in ((4, PLUS), (5, MINUS)):
            if not chunks:
                continue

            @pl.when(c == chunks[0])
            def _():
                wait(tok.at[n - 1], tok_recv.at[n - 1])

            @pl.when(among(c, chunks))
            def _():
                dispatch(n, c)

    for c in range(AHEAD_HAND):
        own_slice(c)

    def drain(c):
        for n in range(4):
            @pl.when(c > 0)
            def _():
                wait(outgoing.at[n, c], x_send.at[n, c])

            @pl.when(c == 0)
            def _():
                part = outgoing.at[n, c, pl.ds(CAP, ROWS - CAP)]
                wait(part, x_send.at[n, c])

        for n, other, chunks in ((4, 1, PLUS), (5, 0, MINUS)):
            @pl.when(among(c, chunks))
            def _():
                wait(outgoing.at[n, c], x_send.at[n, c])

            @pl.when(jnp.logical_not(among(c, chunks)))
            def _():
                wait(x.at[0, c], fwd_send.at[other, c])

        for n in range(2, 4):
            wait(x.at[0, c], fwd_send.at[n, c])
        for n in range(8):
            if n in (5, 7):
                half = hid.at[0, c, pl.ds(0, ROWS // 2)]
                wait(half, hid_send.at[n, c])
            else:
                wait(hid.at[0, c], hid_send.at[n, c])

        @pl.when(c > 0)
        def _():
            wait(res.at[c], ret_send.at[c])

        @pl.when(c == 0)
        def _():
            part = res.at[c, pl.ds(CAP, ROWS - CAP)]
            wait(part, ret_send.at[c])

    def drain_tokens():
        for n in (0, 1) + ((3,) if PLUS else ()) + ((4,) if MINUS else ()):
            wait(tok_in, tok_send.at[n])
        for n in (0, 1):
            half = tok.at[n, pl.ds(n * HALF, HALF)]
            wait(half, half_send.at[n])

    def step(j, _):
        def ahead(lead, do):
            first = jnp.where(j > RAMP, j + lead + 1, j + lead)
            end = jnp.where(j >= RAMP, j + lead + 2, j + lead + 1)

            def one(c, _):
                do(c)
                return 0

            lax.fori_loop(jnp.minimum(first, CHUNKS), jnp.minimum(end, CHUNKS), one, 0)

        def at(lag, do):
            c = j - lag
            pl.when(jnp.logical_and(c >= 0, c < CHUNKS))(lambda: do(c))

        def other_slices(c):
            arrived(2, c)
            hand_on(2, c, -1, 2)
            arrived(6, c)
            hand_on(6, c, 1, 3)

        def dispatch_ahead(c):
            dispatch(1, c)
            dispatch(2, c)

        at(LAG_HALF, second_half)
        at(-AHEAD_HAND, own_slice)
        for early in range(AHEAD_LATE):
            pl.when(j == 0)(functools.partial(dispatch_late, early))
        at(-AHEAD_LATE, dispatch_late)
        at(LAG_HOP4, fourth_hop)
        at(LAG_HOP2, second_hop)
        ahead(AHEAD_OWN, lambda c: dispatch(0, c))
        ahead(AHEAD, dispatch_ahead)
        at(0, other_slices)
        at(LAG_DOWN, down)
        at(0, first_half)
        at(LAG_HOP3, third_hop)
        pl.when(j == CHUNKS)(drain_tokens)
        at(LAG_MIX, drain)
        at(LAG_MIX, combine)
        return 0

    lax.fori_loop(0, CHUNKS + LAG_MIX, step, 0)

    out_ref[...] = mix[...].astype(BF16)


def local(tokens, indices, scores, gate_weight, up_weight, down_weight):
    vmem = pl.BlockSpec(memory_space=pltpu.VMEM)
    anywhere = pl.BlockSpec(memory_space=pl.ANY)
    dma = pltpu.SemaphoreType.DMA
    return pl.pallas_call(
        kernel,
        out_shape=jax.ShapeDtypeStruct((TOK, FEAT), BF16),
        in_specs=[vmem, vmem, vmem, anywhere, anywhere, anywhere],
        out_specs=vmem,
        scratch_shapes=[
            pltpu.VMEM((TP, FEAT, HID), BF16),
            pltpu.VMEM((TP, FEAT, HID), BF16),
            pltpu.VMEM((FEAT, TP * HID), BF16),
            pltpu.VMEM((CHUNKS, ROWS, TOK), BF16),
            pltpu.VMEM((3, CHUNKS, TOK, ROWS), BF16),
            pltpu.VMEM((5, TOK, FEAT), BF16),
            pltpu.VMEM((6, CHUNKS, ROWS, FEAT), BF16),
            pltpu.VMEM((TP, CHUNKS, ROWS, FEAT), BF16),
            pltpu.VMEM((4, ROWS, HID), F32),
            pltpu.VMEM((4, ROWS, HID), F32),
            pltpu.VMEM((TP, CHUNKS, ROWS, HID), BF16),
            pltpu.VMEM((CHUNKS, ROWS, FEAT), BF16),
            pltpu.VMEM((CHUNKS, ROWS, FEAT), BF16),
            pltpu.VMEM((TOK, FEAT), F32),
            dma((3,)),
            dma((5,)),
            dma((5,)),
            dma((2,)),
            dma((2,)),
            dma((6, CHUNKS)),
            dma((TP, CHUNKS)),
            dma((4, CHUNKS)),
            dma((8, CHUNKS)),
            dma((TP, CHUNKS)),
            dma((2, CHUNKS)),
            dma((CHUNKS,)),
            dma((CHUNKS,)),
        ],
        compiler_params=pltpu.CompilerParams(
            collective_id=0, has_side_effects=True, vmem_limit_bytes=58 * 2**20
        ),
        cost_estimate=pl.CostEstimate(flops=12 * 10**9, bytes_accessed=12 * 10**6, transcendentals=1024 * 256),
    )(
        indices.T, scores.T, tokens,
        gate_weight.reshape(TP, FEAT, HID), up_weight.reshape(TP, FEAT, HID), down_weight[0],
    )


def solution(mesh):
    placed = (
        P("ep", "tp"),
        P("ep", None),
        P("ep", None),
        P("ep", None, "tp"),
        P("ep", None, "tp"),
        P("ep", "tp", None),
    )
    return jax.shard_map(
        local, mesh=mesh, in_specs=placed, out_specs=P("ep", "tp"), check_vma=False
    )
```
